256 devices in a mesh: col: 32 (over y, x, core), row: 8 (over z).
Axes of the slice: x: 4, y: 4, z: 8, core: 2. Of those that a mesh axis runs over, the one named last changes fastest.
Arguments:
- rhs: bfloat16 [6, 32, 8, 128, 512], P(None, 'col', 'row'), may hold values from -6 to 6
- diag_inv: bfloat16 [6, 32, 8, 128, 128], P(None, 'col', 'row'), may hold values from -0.5 to 0.5
- factor: bfloat16 [5, 32, 8, 32, 2, 128, 128], P(None, 'col', 'row'), may hold values from -0.125 to 0.125
- columns: int32 [5, 32, 8, 32, 2], P(None, 'col', 'row'), may hold values from 0 to 7, as said below
Outputs:
- solution: bfloat16 [6, 32, 8, 128, 512], P(None, 'col', 'row')
The draws below stay inside these ranges and needn't reach their ends.
Inputs may be any that keep to these rules, and one draw needn't show every extreme that they name: The 2 entries of columns for one factor row block and one column owner are distinct.
All inputs are finite; a program needn't handle non-finite values.
Results may differ from the reference program's by a relative error of at most 0.025.
Values may be sent and summed in bfloat16 or wider, within the bound.
No kernel may reach another device: no remote copies, remote signals or barrier semaphores. Data moves between devices by JAX's collectives and lax.ppermute only.
A program may use at most 128 MiB of HBM per device.

```python
import jax
import jax.numpy as jnp
from jax import lax

BLK = 128
NRHS = 512
STEPS = 6
SLOTS = 2
N_COL = 32
N_ROW = 8


def draw_columns(key, part):
    shape = (STEPS - 1, N_COL, N_ROW, N_COL, N_ROW)
    scores = jax.random.randint(jax.random.fold_in(key, 17), shape, 0, 1000)
    scores = scores * N_ROW + jnp.arange(N_ROW, dtype=jnp.int32)
    order = jnp.argsort(scores, axis=-1)
    return order[..., :SLOTS].astype(jnp.int32)


def spiked(result, stream_key, source, target, parts, factor):
    owner, partner = [(jnp.arange(result.shape[dim]) // (result.shape[dim] // parts)).reshape([-1 if axis == dim else 1 for axis in range(result.ndim)]) for dim in (source, target)]
    chosen = jax.random.permutation(stream_key, parts)[partner]
    strong = (owner == chosen) | (owner == (partner + parts // 2) % parts)
    return jnp.where(strong, factor * result, result)


def levels(stream_key, dims, shards, low, largest):
    level = 1.0
    for position, parts in shards:
        steps = jax.random.uniform(jax.random.fold_in(jax.random.fold_in(stream_key, 6), position), (parts,), jnp.float32, low / len(shards), largest / len(shards))
        level = level * jnp.repeat(jnp.exp(steps), dims[position] // parts).reshape((-1,) + (1,) * (len(dims) - 1 - position))
    return level


def gaussian(rng, extent, spread, most, split=(), kind=jnp.bfloat16):
    loudness = levels(rng, extent, split, -0.22, 0.18) if split else 1.0
    array = jax.random.normal(rng, extent, jnp.float32) * spread * loudness
    return jnp.minimum(jnp.maximum(array, -most), most).astype(kind)


def bell_draw_with(stream_key, dims, spread, bound, shards, heavy, held_as=jnp.bfloat16):
    entries = spread * jax.random.normal(stream_key, dims, jnp.float32)
    if shards:
        entries = entries * levels(stream_key, dims, shards, -0.22, 0.18)
    return jnp.clip(spiked(entries, jax.random.fold_in(stream_key, 3), *heavy), -bound, bound).astype(held_as)


def setup_inputs(seed: int = 0) -> dict:
    key_of = jax.random.split(jax.random.key(seed), 5)
    return {
        "rhs": gaussian(key_of[0], (STEPS, N_COL, N_ROW, BLK, NRHS), 1.0, 6.0, ((1, 32), (2, 8))),
        "diag_inv": gaussian(key_of[1], (STEPS, N_COL, N_ROW, BLK, BLK), BLK ** -0.5, 0.5, ((1, 32), (2, 8))),
        "factor": bell_draw_with(key_of[2], (STEPS - 1, N_COL, N_ROW, N_COL, SLOTS, BLK, BLK), (N_COL * SLOTS * BLK) ** -0.5, 0.125, ((1, 32), (2, 8)), (1, 3, 32, 2.75)),
        "columns": draw_columns(jax.random.fold_in(key_of[4], 71), 0),
    }


def reference(rhs, diag_inv, factor, columns):
    highest = lax.Precision.HIGHEST
    remainder = rhs[0].astype(jnp.float32)
    solved = []
    for step_index in range(STEPS):
        current = jnp.einsum('crab,crbn->cran', diag_inv[step_index].astype(jnp.float32), remainder, precision=highest).astype(jnp.bfloat16)
        solved.append(current)
        if step_index + 1 < STEPS:
            def add_owner(carry, inputs):
                blocks, selected, panels = inputs
                chosen = jnp.take(panels, selected, axis=0).astype(jnp.float32)
                part_sum = jnp.einsum('rtmab,rtmbn->rtan', blocks.astype(jnp.float32), chosen, precision=highest)
                rounded = lax.optimization_barrier(part_sum.astype(jnp.bfloat16))
                return carry + rounded.astype(jnp.float32), None

            start_sum = jnp.zeros((N_ROW, N_COL, BLK, NRHS), jnp.float32)
            total, unused = lax.scan(add_owner, start_sum, (factor[step_index], columns[step_index], current))
            remainder = rhs[step_index + 1].astype(jnp.float32) - jnp.transpose(total, (1, 0, 2, 3))
    return jnp.stack(solved)
```

```python
import functools

import jax
import jax.numpy as jnp
from jax import lax
from jax.experimental import pallas as pl
from jax.experimental.pallas import tpu as pltpu
from jax.sharding import Mesh
from jax.sharding import PartitionSpec as P

CORES = 2
TARGET_BLOCK = 8
SOURCE_BLOCK = 4
VMEM_LIMIT = 40 * 1024 * 1024


def times_inverse(inverse, remainder):
    high = remainder.astype(jnp.bfloat16)
    rest = remainder - high.astype(jnp.float32)
    middle = rest.astype(jnp.bfloat16)
    low = (rest - middle.astype(jnp.float32)).astype(jnp.bfloat16)
    dot = functools.partial(jnp.dot, inverse, preferred_element_type=jnp.float32)
    return (dot(low) + dot(middle) + dot(high)).astype(jnp.bfloat16)


def store_solved(mine, other, inv_mine, inv_other, copies_ref, solved_ref):
    for slot, (remainder, inverse) in enumerate(((mine, inv_mine), (other, inv_other))):
        panel = times_inverse(inverse, remainder)
        solved_ref[slot] = panel
        for peer in range(copies_ref.shape[0]):
            copies_ref[peer, slot] = panel


def first_kernel(core_ref, rhs_ref, rhs_other_ref, inv_ref, inv_other_ref, copies_ref, solved_ref):
    store_solved(
        rhs_ref[0, 0, 0].astype(jnp.float32),
        rhs_other_ref[0].astype(jnp.float32),
        inv_ref[0, 0, 0],
        inv_other_ref[0, 0, 0],
        copies_ref,
        solved_ref,
    )


def next_kernel(
    core_ref, terms_ref, rhs_ref, rhs_other_ref, inv_ref, inv_other_ref, copies_ref, solved_ref, total
):
    step = pl.program_id(0)
    part = jnp.sum(terms_ref[...].astype(jnp.float32), axis=0)

    @pl.when(step == 0)
    def _():
        total[...] = part

    @pl.when(step > 0)
    def _():
        total[...] += part

    @pl.when(step == pl.num_programs(0) - 1)
    def _():
        store_solved(
            rhs_ref[0, 0, 0].astype(jnp.float32) - total[0],
            rhs_other_ref[0].astype(jnp.float32) - total[1],
            inv_ref[0, 0, 0],
            inv_other_ref[0, 0, 0],
            copies_ref,
            solved_ref,
        )


def solve(level, core, terms, rhs, rhs_other, inv, inv_other, peers):
    _, _, _, blk, width = rhs.shape
    half = width // CORES
    steps = 1 if terms is None else terms.shape[0] // SOURCE_BLOCK
    level_specs = [
        pl.BlockSpec((1, 1, 1, blk, half), lambda i, c: (level, 0, 0, 0, c[0])),
        pl.BlockSpec((1, blk, half), lambda i, c: (level, 0, 0)),
        pl.BlockSpec((1, 1, 1, blk, blk), lambda i, c: (level, 0, 0, 0, 0)),
        pl.BlockSpec((1, 1, 1, blk, blk), lambda i, c: (level, 0, 0, 0, 0)),
    ]
    term_specs = [pl.BlockSpec((SOURCE_BLOCK, CORES, blk, half), lambda i, c: (i, 0, 0, 0))]
    operands = (rhs, rhs_other, inv, inv_other)
    return pl.pallas_call(
        first_kernel if terms is None else next_kernel,
        out_shape=(
            jax.ShapeDtypeStruct((peers, CORES, blk, half), jnp.bfloat16),
            jax.ShapeDtypeStruct((CORES, blk, half), jnp.bfloat16),
        ),
        grid_spec=pltpu.PrefetchScalarGridSpec(
            num_scalar_prefetch=1,
            grid=(steps,),
            in_specs=level_specs if terms is None else term_specs + level_specs,
            out_specs=(
                pl.BlockSpec((peers, CORES, blk, half), lambda i, c: (0, 0, 0, 0)),
                pl.BlockSpec((CORES, blk, half), lambda i, c: (0, 0, 0)),
            ),
            scratch_shapes=[] if terms is None else [pltpu.VMEM((CORES, blk, half), jnp.float32)],
        ),
        compiler_params=pltpu.CompilerParams(vmem_limit_bytes=VMEM_LIMIT),
        name="solve_panels",
    )(core, *(operands if terms is None else (terms, *operands)))


def terms_kernel(level, slots, core_ref, cols_ref, cols_other_ref, panels_ref, mine_ref, other_ref, out_ref):
    core = core_ref[0]
    step = pl.program_id(0)
    block = mine_ref.shape[3]
    targets = block * pl.num_programs(0)
    for chip in range(block // CORES):
        for slot in range(CORES):
            local = CORES * chip + (core if slot == 0 else 1 - core)
            place = (level * targets + step * block + local) * slots
            left, right = [], []
            for which, (blocks, cols) in enumerate(((mine_ref, cols_ref), (other_ref, cols_other_ref))):
                for m in range(slots):
                    left.append(blocks[0, 0, 0, local, m])
                    right.append(panels_ref[cols[place + m], which])
            product = jnp.dot(
                jnp.concatenate(left, axis=1),
                jnp.concatenate(right, axis=0),
                preferred_element_type=jnp.float32,
            )
            out_ref[chip, slot] = product.astype(jnp.bfloat16)


def terms(level, core, cols, cols_other, panels, factor, factor_other):
    _, _, _, targets, slots, blk, _ = factor.shape
    half = panels.shape[-1]
    factor_spec = pl.BlockSpec(
        (1, 1, 1, TARGET_BLOCK, slots, blk, blk), lambda i, *_: (level, 0, 0, i, 0, 0, 0)
    )
    return pl.pallas_call(
        functools.partial(terms_kernel, level, slots),
        out_shape=jax.ShapeDtypeStruct((targets // CORES, CORES, blk, half), jnp.bfloat16),
        grid_spec=pltpu.PrefetchScalarGridSpec(
            num_scalar_prefetch=3,
            grid=(targets // TARGET_BLOCK,),
            in_specs=[
                pl.BlockSpec(panels.shape, lambda i, *_: (0, 0, 0, 0)),
                factor_spec,
                factor_spec,
            ],
            out_specs=pl.BlockSpec(
                (TARGET_BLOCK // CORES, CORES, blk, half), lambda i, *_: (i, 0, 0, 0)
            ),
        ),
        compiler_params=pltpu.CompilerParams(vmem_limit_bytes=VMEM_LIMIT),
        name="level_terms",
    )(core, cols, cols_other, panels, factor, factor_other)


def on_device(rhs, diag_inv, factor, columns):
    levels = rhs.shape[0]
    half = rhs.shape[-1] // CORES
    peers = lax.axis_size("row")
    here = lax.axis_index("core").astype(jnp.int32)
    core = here.reshape(1)
    swap = functools.partial(lax.ppermute, axis_name="core", perm=[(0, 1), (1, 0)])

    theirs = lax.dynamic_slice_in_dim(rhs[:, 0, 0], (1 - here) * half, half, axis=2)
    rhs_other = swap(theirs)
    inv_other = swap(diag_inv)
    cols = columns.reshape(-1)
    cols_other = swap(cols)
    factor_other = swap(factor)

    solved = []
    received = None
    for level in range(levels):
        copies, panel = solve(level, core, received, rhs, rhs_other, diag_inv, inv_other, peers)
        solved.append(panel)
        if level + 1 < levels:
            panels = lax.all_to_all(copies, "row", 0, 0, tiled=True)
            partial = terms(level, core, cols, cols_other, panels, factor, factor_other)
            received = lax.all_to_all(partial, "chip", 0, 0, tiled=True)

    def whole(panels):
        mine = jnp.stack([p[0] for p in panels])
        other = swap(jnp.stack([p[1] for p in panels]))
        return jnp.where(
            here == 0,
            jnp.concatenate([mine, other], axis=-1),
            jnp.concatenate([other, mine], axis=-1),
        )

    out = jnp.concatenate([whole(solved[:-1]), whole(solved[-1:])], axis=0)
    return out[:, None, None]


def solution(mesh):
    cols, rows = mesh.devices.shape
    fine = Mesh(mesh.devices.reshape(cols // CORES, CORES, rows), ("chip", "core", "row"))
    owner = ("chip", "core")
    return jax.shard_map(
        on_device,
        mesh=fine,
        in_specs=(
            P(None, owner, "row", None, None),
            P(None, owner, "row", None, None),
            P(None, owner, "row", None, None, None, None),
            P(None, owner, "row", None, None),
        ),
        out_specs=P(None, owner, "row", None, None),
        check_vma=False,
    )
```

```python
import functools

import jax
import jax.numpy as jnp
from jax import lax
from jax.experimental import pallas as pl
from jax.experimental.pallas import tpu as pltpu
from jax.sharding import Mesh
from jax.sharding import PartitionSpec as P

CORES = 2
CHIP_BLOCK = 4
STAGGER = 36
VMEM_LIMIT = 16 * 1024 * 1024
VMEM = pl.BlockSpec(memory_space=pltpu.VMEM)
SMEM = pl.BlockSpec(memory_space=pltpu.SMEM)
PARAMS = pltpu.CompilerParams(vmem_limit_bytes=VMEM_LIMIT)


def times_inverse(inverse, remainder):
    high = remainder.astype(jnp.bfloat16)
    rest = remainder - high.astype(jnp.float32)
    middle = rest.astype(jnp.bfloat16)
    low = (rest - middle.astype(jnp.float32)).astype(jnp.bfloat16)
    dot = functools.partial(jnp.dot, inverse, preferred_element_type=jnp.float32)
    return (dot(low) + dot(middle) + dot(high)).astype(jnp.bfloat16)


def store_solved(slot, inverse, remainder, copies_ref, solved_ref):
    panel = times_inverse(inverse, remainder)
    solved_ref[slot] = panel
    for peer in range(copies_ref.shape[0]):
        copies_ref[peer, slot] = panel


def first_kernel(core_ref, rhs_ref, inv_ref, copies_ref, solved_ref):
    def once(_, carry):
        for slot in range(CORES):
            store_solved(
                slot, inv_ref[slot], rhs_ref[slot].astype(jnp.float32), copies_ref, solved_ref
            )
        return carry

    lax.fori_loop(0, 1 + (1 - core_ref[0]) * STAGGER, once, 0)


def next_kernel(terms_ref, rhs_ref, inv_ref, *out_refs):
    for slot in range(CORES):
        total = terms_ref[0, slot].astype(jnp.float32)
        for chip in range(1, terms_ref.shape[0]):
            total += terms_ref[chip, slot].astype(jnp.float32)
        remainder = rhs_ref[slot].astype(jnp.float32) - total
        if len(out_refs) == 2:
            store_solved(slot, inv_ref[slot], remainder, *out_refs)
        else:
            out_refs[0][slot] = times_inverse(inv_ref[slot], remainder)


def solve(core, terms, rhs, inv, peers):
    solved = jax.ShapeDtypeStruct(rhs.shape, jnp.bfloat16)
    copies = jax.ShapeDtypeStruct((peers, *rhs.shape), jnp.bfloat16)
    if terms is None:
        return pl.pallas_call(
            first_kernel,
            out_shape=(copies, solved),
            in_specs=[SMEM, VMEM, VMEM],
            out_specs=(VMEM, VMEM),
            compiler_params=PARAMS,
            name="first_panels",
        )(core, rhs, inv)
    return pl.pallas_call(
        next_kernel,
        out_shape=(copies, solved) if peers else solved,
        in_specs=[VMEM, VMEM, VMEM],
        out_specs=(VMEM, VMEM) if peers else VMEM,
        compiler_params=PARAMS,
        name="solve_panels",
    )(terms, rhs, inv)


def terms_kernel(level, core_ref, cols_ref, cols_other_ref, panels_ref, mine_ref, other_ref, out_ref):
    core = core_ref[0]
    targets, slots = mine_ref.shape[:2]

    def some_chips(block, carry):
        for chip in range(CHIP_BLOCK):
            for slot in range(CORES):
                target = CORES * (block * CHIP_BLOCK + chip) + (core if slot == 0 else 1 - core)
                place = (level * targets + target) * slots
                left, right = [], []
                for which, (blocks, cols) in enumerate(
                    ((mine_ref, cols_ref), (other_ref, cols_other_ref))
                ):
                    for m in range(slots):
                        left.append(blocks[target, m])
                        right.append(panels_ref[cols[place + m], which])
                product = jnp.dot(
                    jnp.concatenate(left, axis=1),
                    jnp.concatenate(right, axis=0),
                    preferred_element_type=jnp.float32,
                )
                out_ref[block * CHIP_BLOCK + chip, slot] = product.astype(jnp.bfloat16)
        return carry

    lax.fori_loop(0, targets // CORES // CHIP_BLOCK, some_chips, 0)


def terms(level, core, cols, cols_other, panels, mine, other):
    targets = mine.shape[0]
    return pl.pallas_call(
        functools.partial(terms_kernel, level),
        out_shape=jax.ShapeDtypeStruct((targets // CORES, *panels.shape[1:]), jnp.bfloat16),
        in_specs=[SMEM, SMEM, SMEM, VMEM, VMEM, VMEM],
        out_specs=VMEM,
        compiler_params=PARAMS,
        name="level_terms",
    )(core, cols, cols_other, panels, mine, other)


def on_device(rhs, diag_inv, factor, columns):
    levels = rhs.shape[0]
    half = rhs.shape[-1] // CORES
    peers = lax.axis_size("row")
    here = lax.axis_index("core").astype(jnp.int32)
    core = here.reshape(1)
    swap = functools.partial(lax.ppermute, axis_name="core", perm=[(0, 1), (1, 0)])

    rhs_here = lax.dynamic_slice_in_dim(rhs[:, 0, 0], here * half, half, axis=2)
    rhs_other = swap(lax.dynamic_slice_in_dim(rhs[:, 0, 0], (1 - here) * half, half, axis=2))
    inv_other = swap(diag_inv)
    columns_other = swap(columns)
    large, rhs_other, inv_other, columns_other = lax.optimization_barrier(
        (factor, rhs_other, inv_other, columns_other)
    )
    factor_other = swap(large)
    rhs_pair = jnp.stack([rhs_here, rhs_other], axis=1)
    inv_pair = jnp.stack([diag_inv[:, 0, 0], inv_other[:, 0, 0]], axis=1)
    cols, cols_other = columns.reshape(-1), columns_other.reshape(-1)

    solved = []
    received = None
    for level in range(levels):
        last = level + 1 == levels
        result = solve(core, received, rhs_pair[level], inv_pair[level], 0 if last else peers)
        if last:
            solved.append(result)
            break
        copies, panel = result
        solved.append(panel)
        panels = lax.all_to_all(copies, "row", 0, 0, tiled=True)
        partial = terms(
            level, core, cols, cols_other, panels, factor[level, 0, 0], factor_other[level, 0, 0]
        )
        received = lax.all_to_all(partial, "chip", 0, 0, tiled=True)

    def whole(panels):
        mine = jnp.stack([p[0] for p in panels])
        other = swap(jnp.stack([p[1] for p in panels]))
        return jnp.where(
            here == 0,
            jnp.concatenate([mine, other], axis=-1),
            jnp.concatenate([other, mine], axis=-1),
        )

    out = jnp.concatenate([whole(solved[:-1]), whole(solved[-1:])], axis=0)
    return out[:, None, None]


def solution(mesh):
    cols, rows = mesh.devices.shape
    fine = Mesh(mesh.devices.reshape(cols // CORES, CORES, rows), ("chip", "core", "row"))
    owner = ("chip", "core")
    return jax.shard_map(
        on_device,
        mesh=fine,
        in_specs=(
            P(None, owner, "row", None, None),
            P(None, owner, "row", None, None),
            P(None, owner, "row", None, None, None, None),
            P(None, owner, "row", None, None),
        ),
        out_specs=P(None, owner, "row", None, None),
        check_vma=False,
    )
```

```python
import functools

import jax
import jax.numpy as jnp
from jax import lax
from jax.experimental import pallas as pl
from jax.experimental.pallas import tpu as pltpu
from jax.sharding import Mesh
from jax.sharding import PartitionSpec as P

CORES = 2
CHIP_BLOCK = 8
STAGGER = 36
VMEM_LIMIT = 16 * 1024 * 1024
VMEM = pl.BlockSpec(memory_space=pltpu.VMEM)
SMEM = pl.BlockSpec(memory_space=pltpu.SMEM)
PARAMS = pltpu.CompilerParams(vmem_limit_bytes=VMEM_LIMIT)


def times_inverse(inverse, remainder):
    high = remainder.astype(jnp.bfloat16)
    rest = remainder - high.astype(jnp.float32)
    middle = rest.astype(jnp.bfloat16)
    low = (rest - middle.astype(jnp.float32)).astype(jnp.bfloat16)
    dot = functools.partial(jnp.dot, inverse, preferred_element_type=jnp.float32)
    return (dot(low) + dot(middle) + dot(high)).astype(jnp.bfloat16)


def store_solved(level, slot, inverse, remainder, solved_ref, copies_ref):
    panel = times_inverse(inverse, remainder)
    solved_ref[level] = panel
    if copies_ref is not None:
        for peer in range(copies_ref.shape[0]):
            copies_ref[peer, slot] = panel


def first_kernel(core_ref, rhs_ref, inv_ref, mine_ref, other_ref, copies_ref):
    def once(_, carry):
        for slot, solved_ref in enumerate((mine_ref, other_ref)):
            remainder = rhs_ref[slot].astype(jnp.float32)
            store_solved(0, slot, inv_ref[slot], remainder, solved_ref, copies_ref)
        return carry

    lax.fori_loop(0, 1 + (1 - core_ref[0]) * STAGGER, once, 0)


def next_kernel(level, terms_ref, *refs):
    rhs_refs, inv_refs, solved_refs = refs[:2], refs[2:4], refs[6:8]
    copies_ref = refs[8] if len(refs) > 8 else None
    for slot in range(CORES):
        total = terms_ref[0, slot].astype(jnp.float32)
        for chip in range(1, terms_ref.shape[0]):
            total += terms_ref[chip, slot].astype(jnp.float32)
        remainder = rhs_refs[slot][level].astype(jnp.float32) - total
        store_solved(level, slot, inv_refs[slot][level], remainder, solved_refs[slot], copies_ref)


def first_solve(core, rhs, inv, levels, peers):
    solved = jax.ShapeDtypeStruct((levels, *rhs.shape[1:]), jnp.bfloat16)
    return pl.pallas_call(
        first_kernel,
        out_shape=(solved, solved, jax.ShapeDtypeStruct((peers, *rhs.shape), jnp.bfloat16)),
        in_specs=[SMEM, VMEM, VMEM],
        out_specs=(VMEM, VMEM, VMEM),
        compiler_params=PARAMS,
        name="first_panels",
    )(core, rhs, inv)


def solve(level, received, rhs, inv, solved, peers):
    outs = [jax.ShapeDtypeStruct(x.shape, x.dtype) for x in solved]
    if peers:
        outs.append(jax.ShapeDtypeStruct((peers, *received.shape[1:]), jnp.bfloat16))
    result = pl.pallas_call(
        functools.partial(next_kernel, level),
        out_shape=tuple(outs),
        in_specs=[VMEM] * 7,
        out_specs=(VMEM,) * len(outs),
        input_output_aliases={5: 0, 6: 1},
        compiler_params=PARAMS,
        name="solve_panels",
    )(received, *rhs, *inv, *solved)
    return result[:2], result[2] if peers else None


def terms_kernel(level, core_ref, cols_ref, cols_other_ref, panels_ref, mine_ref, other_ref, out_ref):
    core = core_ref[0]
    targets, slots = mine_ref.shape[:2]

    def some_chips(block, carry):
        for chip in range(CHIP_BLOCK):
            for slot in range(CORES):
                target = CORES * (block * CHIP_BLOCK + chip) + (core if slot == 0 else 1 - core)
                place = (level * targets + target) * slots
                left, right = [], []
                for which, (blocks, cols) in enumerate(
                    ((mine_ref, cols_ref), (other_ref, cols_other_ref))
                ):
                    for m in range(slots):
                        left.append(blocks[target, m])
                        right.append(panels_ref[cols[place + m], which])
                product = jnp.dot(
                    jnp.concatenate(left, axis=1),
                    jnp.concatenate(right, axis=0),
                    preferred_element_type=jnp.float32,
                )
                out_ref[block * CHIP_BLOCK + chip, slot] = product.astype(jnp.bfloat16)
        return carry

    lax.fori_loop(0, targets // CORES // CHIP_BLOCK, some_chips, 0)


def terms(level, core, cols, cols_other, panels, mine, other):
    targets = mine.shape[0]
    return pl.pallas_call(
        functools.partial(terms_kernel, level),
        out_shape=jax.ShapeDtypeStruct((targets // CORES, *panels.shape[1:]), jnp.bfloat16),
        in_specs=[SMEM, SMEM, SMEM, VMEM, VMEM, VMEM],
        out_specs=VMEM,
        compiler_params=PARAMS,
        name="level_terms",
    )(core, cols, cols_other, panels, mine, other)


def on_device(rhs, diag_inv, factor, columns):
    levels = rhs.shape[0]
    half = rhs.shape[-1] // CORES
    peers = lax.axis_size("row")
    here = lax.axis_index("core").astype(jnp.int32)
    core = here.reshape(1)
    swap = functools.partial(lax.ppermute, axis_name="core", perm=[(0, 1), (1, 0)])

    rhs_here = lax.dynamic_slice_in_dim(rhs[:, 0, 0], here * half, half, axis=2)
    rhs_other = swap(lax.dynamic_slice_in_dim(rhs[:, 0, 0], (1 - here) * half, half, axis=2))
    inv_other = swap(diag_inv)
    columns_other = swap(columns)
    large, rhs_other, inv_other, columns_other = lax.optimization_barrier(
        (factor, rhs_other, inv_other, columns_other)
    )
    factor_other = swap(large)
    cols, cols_other = columns.reshape(-1), columns_other.reshape(-1)
    rhs_all = (rhs_here, rhs_other)
    inv_all = (diag_inv[:, 0, 0], inv_other[:, 0, 0])

    mine, other, copies = first_solve(
        core, jnp.stack([x[0] for x in rhs_all]), jnp.stack([x[0] for x in inv_all]), levels, peers
    )
    solved = (mine, other)
    first_factors = factor[0, 0, 0], factor_other[0, 0, 0]
    for level in range(levels - 1):
        panels = lax.all_to_all(copies, "row", 0, 0, tiled=True)
        factors = (
            (factor[level, 0, 0], factor_other[level, 0, 0]) if level else first_factors
        )
        partial = terms(level, core, cols, cols_other, panels, *factors)
        received = lax.all_to_all(partial, "chip", 0, 0, tiled=True)
        last = level + 2 == levels
        solved, copies = solve(level + 1, received, rhs_all, inv_all, solved, 0 if last else peers)

    mine, other = solved[0], swap(solved[1])
    out = jnp.where(
        here == 0,
        jnp.concatenate([mine, other], axis=-1),
        jnp.concatenate([other, mine], axis=-1),
    )
    return out[:, None, None]


def solution(mesh):
    cols, rows = mesh.devices.shape
    fine = Mesh(mesh.devices.reshape(cols // CORES, CORES, rows), ("chip", "core", "row"))
    owner = ("chip", "core")
    return jax.shard_map(
        on_device,
        mesh=fine,
        in_specs=(
            P(None, owner, "row", None, None),
            P(None, owner, "row", None, None),
            P(None, owner, "row", None, None, None, None),
            P(None, owner, "row", None, None),
        ),
        out_specs=P(None, owner, "row", None, None),
        check_vma=False,
    )
```

```python
import functools

import jax
import jax.numpy as jnp
from jax import lax
from jax.experimental import pallas as pl
from jax.experimental.pallas import tpu as pltpu
from jax.sharding import Mesh
from jax.sharding import PartitionSpec as P

CORES = 2
RING_PARTS = 2
CHIP_BLOCK = 16
STAGGER = 36
VMEM_LIMIT = 16 * 1024 * 1024
VMEM = pl.BlockSpec(memory_space=pltpu.VMEM)
SMEM = pl.BlockSpec(memory_space=pltpu.SMEM)
PARAMS = pltpu.CompilerParams(vmem_limit_bytes=VMEM_LIMIT)


def times_inverse(inverse, remainder):
    high = remainder.astype(jnp.bfloat16)
    rest = remainder - high.astype(jnp.float32)
    middle = rest.astype(jnp.bfloat16)
    low = (rest - middle.astype(jnp.float32)).astype(jnp.bfloat16)
    dot = functools.partial(jnp.dot, inverse, preferred_element_type=jnp.float32)
    return (dot(low) + dot(middle) + dot(high)).astype(jnp.bfloat16)


def store_solved(level, slot, inverse, remainder, solved_ref, copies_ref):
    panel = times_inverse(inverse, remainder)
    solved_ref[level] = panel
    if copies_ref is not None:
        for peer in range(copies_ref.shape[0]):
            copies_ref[peer, slot] = panel


def first_kernel(core_ref, given_ref, mine_ref, other_ref, copies_ref):
    def once(_, carry):
        for slot, solved_ref in enumerate((mine_ref, other_ref)):
            half = solved_ref.shape[-1]
            remainder = given_ref[slot, :, :half].astype(jnp.float32)
            store_solved(0, slot, given_ref[slot, :, half:], remainder, solved_ref, copies_ref)
        return carry

    lax.fori_loop(0, 1 + (1 - core_ref[0]) * STAGGER, once, 0)


def next_kernel(level, terms_ref, *refs):
    rhs_refs, inv_refs, solved_refs = refs[:2], refs[2:4], refs[6:8]
    copies_ref = refs[8] if len(refs) > 8 else None
    for slot in range(CORES):
        total = terms_ref[0, slot].astype(jnp.float32)
        for chip in range(1, terms_ref.shape[0]):
            total += terms_ref[chip, slot].astype(jnp.float32)
        remainder = rhs_refs[slot][level].astype(jnp.float32) - total
        store_solved(level, slot, inv_refs[slot][level], remainder, solved_refs[slot], copies_ref)


def first_solve(core, given, levels, peers):
    _, blk, width = given.shape
    half = width - blk
    solved = jax.ShapeDtypeStruct((levels, blk, half), jnp.bfloat16)
    return pl.pallas_call(
        first_kernel,
        out_shape=(
            solved,
            solved,
            jax.ShapeDtypeStruct((peers, CORES, blk, half), jnp.bfloat16),
        ),
        in_specs=[SMEM, VMEM],
        out_specs=(VMEM, VMEM, VMEM),
        compiler_params=PARAMS,
        name="first_panels",
    )(core, given)


def solve(level, received, rhs, inv, solved, peers):
    outs = [jax.ShapeDtypeStruct(x.shape, x.dtype) for x in solved]
    if peers:
        outs.append(jax.ShapeDtypeStruct((peers, *received.shape[1:]), jnp.bfloat16))
    result = pl.pallas_call(
        functools.partial(next_kernel, level),
        out_shape=tuple(outs),
        in_specs=[VMEM] * 7,
        out_specs=(VMEM,) * len(outs),
        input_output_aliases={5: 0, 6: 1},
        compiler_params=PARAMS,
        name="solve_panels",
    )(received, *rhs, *inv, *solved)
    return result[:2], result[2] if peers else None


def terms_kernel(level, core_ref, cols_ref, cols_other_ref, panels_ref, mine_ref, other_ref, out_ref):
    core = core_ref[0]
    targets, slots = mine_ref.shape[:2]

    def some_chips(block, carry):
        for chip in range(CHIP_BLOCK):
            for slot in range(CORES):
                target = CORES * (block * CHIP_BLOCK + chip) + (core if slot == 0 else 1 - core)
                place = (level * targets + target) * slots
                left, right = [], []
                for which, (blocks, cols) in enumerate(
                    ((mine_ref, cols_ref), (other_ref, cols_other_ref))
                ):
                    for m in range(slots):
                        left.append(blocks[target, m])
                        right.append(panels_ref[cols[place + m], which])
                product = jnp.dot(
                    jnp.concatenate(left, axis=1),
                    jnp.concatenate(right, axis=0),
                    preferred_element_type=jnp.float32,
                )
                out_ref[block * CHIP_BLOCK + chip, slot] = product.astype(jnp.bfloat16)
        return carry

    lax.fori_loop(0, targets // CORES // CHIP_BLOCK, some_chips, 0)


def terms(level, core, cols, cols_other, panels, mine, other):
    targets = mine.shape[0]
    return pl.pallas_call(
        functools.partial(terms_kernel, level),
        out_shape=jax.ShapeDtypeStruct((targets // CORES, *panels.shape[1:]), jnp.bfloat16),
        in_specs=[SMEM, SMEM, SMEM, VMEM, VMEM, VMEM],
        out_specs=VMEM,
        compiler_params=PARAMS,
        name="level_terms",
    )(core, cols, cols_other, panels, mine, other)


def on_device(rhs, diag_inv, factor, columns):
    levels = rhs.shape[0]
    half = rhs.shape[-1] // CORES
    peers = lax.axis_size("row")
    here = lax.axis_index("core").astype(jnp.int32)
    core = here.reshape(1)
    swap = functools.partial(lax.ppermute, axis_name="core", perm=[(0, 1), (1, 0)])

    rhs_here = lax.dynamic_slice_in_dim(rhs[:, 0, 0], here * half, half, axis=2)
    rhs_other = swap(lax.dynamic_slice_in_dim(rhs[:, 0, 0], (1 - here) * half, half, axis=2))
    inv_other = swap(diag_inv)
    columns_other = swap(columns)
    large, rhs_other, inv_other, columns_other = lax.optimization_barrier(
        (factor, rhs_other, inv_other, columns_other)
    )
    factor_other = swap(large)
    ring = peers // RING_PARTS
    order = [part * ring + i for i in range(ring) for part in range(RING_PARTS)]
    cols, cols_other = (
        (x % ring * RING_PARTS + x // ring).reshape(-1) for x in (columns, columns_other)
    )
    rhs_all = (rhs_here, rhs_other)
    inv_all = (diag_inv[:, 0, 0], inv_other[:, 0, 0])

    first = [(x[0], y[0]) for x, y in zip(rhs_all, inv_all)]
    mine, other, copies = first_solve(
        core, jnp.stack([jnp.concatenate(x, axis=1) for x in first]), levels, peers
    )
    solved = (mine, other)
    first_factors = factor[0, 0, 0], factor_other[0, 0, 0]
    for level in range(levels - 1):
        panels = lax.all_to_all(
            copies, "row", 0, 0, axis_index_groups=[order], tiled=True
        )
        factors = (
            (factor[level, 0, 0], factor_other[level, 0, 0]) if level else first_factors
        )
        partial = terms(level, core, cols, cols_other, panels, *factors)
        received = lax.all_to_all(partial, "chip", 0, 0, tiled=True)
        last = level + 2 == levels
        solved, copies = solve(level + 1, received, rhs_all, inv_all, solved, 0 if last else peers)

    mine, other = solved[0], swap(solved[1])
    out = jnp.where(
        here == 0,
        jnp.concatenate([mine, other], axis=-1),
        jnp.concatenate([other, mine], axis=-1),
    )
    return out[:, None, None]


def solution(mesh):
    cols, rows = mesh.devices.shape
    fine = Mesh(mesh.devices.reshape(cols // CORES, CORES, rows), ("chip", "core", "row"))
    owner = ("chip", "core")
    return jax.shard_map(
        on_device,
        mesh=fine,
        in_specs=(
            P(None, owner, "row", None, None),
            P(None, owner, "row", None, None),
            P(None, owner, "row", None, None, None, None),
            P(None, owner, "row", None, None),
        ),
        out_specs=P(None, owner, "row", None, None),
        check_vma=False,
    )
```

```python
import functools

import jax
import jax.numpy as jnp
from jax import lax
from jax.experimental import pallas as pl
from jax.experimental.pallas import tpu as pltpu
from jax.sharding import Mesh
from jax.sharding import PartitionSpec as P

CORES = 2
RING_PARTS = 2
CHIP_BLOCK = 16
STAGGER = 32
VMEM_LIMIT = 16 * 1024 * 1024
VMEM = pl.BlockSpec(memory_space=pltpu.VMEM)
SMEM = pl.BlockSpec(memory_space=pltpu.SMEM)
PARAMS = pltpu.CompilerParams(vmem_limit_bytes=VMEM_LIMIT)


def times_inverse(inverse, remainder):
    high = remainder.astype(jnp.bfloat16)
    rest = remainder - high.astype(jnp.float32)
    middle = rest.astype(jnp.bfloat16)
    low = (rest - middle.astype(jnp.float32)).astype(jnp.bfloat16)
    dot = functools.partial(jnp.dot, inverse, preferred_element_type=jnp.float32)
    return (dot(low) + dot(middle) + dot(high)).astype(jnp.bfloat16)


def store_solved(level, slot, inverse, remainder, solved_ref, copies_ref):
    panel = times_inverse(inverse, remainder)
    solved_ref[level] = panel
    if copies_ref is not None:
        for peer in range(copies_ref.shape[0]):
            copies_ref[peer, slot] = panel


def first_kernel(core_ref, given_ref, mine_ref, other_ref, copies_ref):
    def once(_, carry):
        for slot, solved_ref in enumerate((mine_ref, other_ref)):
            half = solved_ref.shape[-1]
            remainder = given_ref[slot, :, :half].astype(jnp.float32)
            store_solved(0, slot, given_ref[slot, :, half:], remainder, solved_ref, copies_ref)
        return carry

    lax.fori_loop(0, 1 + (1 - core_ref[0]) * STAGGER, once, 0)


def next_kernel(level, terms_ref, *refs):
    rhs_refs, inv_refs, solved_refs = refs[:2], refs[2:4], refs[6:8]
    copies_ref = refs[8] if len(refs) > 8 else None
    for slot in range(CORES):
        total = terms_ref[0, slot].astype(jnp.float32)
        for chip in range(1, terms_ref.shape[0]):
            total += terms_ref[chip, slot].astype(jnp.float32)
        remainder = rhs_refs[slot][level].astype(jnp.float32) - total
        store_solved(level, slot, inv_refs[slot][level], remainder, solved_refs[slot], copies_ref)


def first_solve(core, given, levels, peers):
    _, blk, width = given.shape
    half = width - blk
    solved = jax.ShapeDtypeStruct((levels, blk, half), jnp.bfloat16)
    return pl.pallas_call(
        first_kernel,
        out_shape=(
            solved,
            solved,
            jax.ShapeDtypeStruct((peers, CORES, blk, half), jnp.bfloat16),
        ),
        in_specs=[SMEM, VMEM],
        out_specs=(VMEM, VMEM, VMEM),
        compiler_params=PARAMS,
        name="first_panels",
    )(core, given)


def solve(level, received, rhs, inv, solved, peers):
    outs = [jax.ShapeDtypeStruct(x.shape, x.dtype) for x in solved]
    if peers:
        outs.append(jax.ShapeDtypeStruct((peers, *received.shape[1:]), jnp.bfloat16))
    result = pl.pallas_call(
        functools.partial(next_kernel, level),
        out_shape=tuple(outs),
        in_specs=[VMEM] * 7,
        out_specs=(VMEM,) * len(outs),
        input_output_aliases={5: 0, 6: 1},
        compiler_params=PARAMS,
        name="solve_panels",
    )(received, *rhs, *inv, *solved)
    return result[:2], result[2] if peers else None


def terms_kernel(level, core_ref, cols_ref, cols_other_ref, panels_ref, mine_ref, other_ref, out_ref):
    core = core_ref[0]
    targets, slots = mine_ref.shape[:2]

    def some_chips(block, carry):
        for chip in range(CHIP_BLOCK):
            for slot in range(CORES):
                target = CORES * (block * CHIP_BLOCK + chip) + (core if slot == 0 else 1 - core)
                place = (level * targets + target) * slots
                left, right = [], []
                for which, (blocks, cols) in enumerate(
                    ((mine_ref, cols_ref), (other_ref, cols_other_ref))
                ):
                    for m in range(slots):
                        left.append(blocks[target, m])
                        right.append(panels_ref[cols[place + m], which])
                product = jnp.dot(
                    jnp.concatenate(left, axis=1),
                    jnp.concatenate(right, axis=0),
                    preferred_element_type=jnp.float32,
                )
                out_ref[block * CHIP_BLOCK + chip, slot] = product.astype(jnp.bfloat16)
        return carry

    lax.fori_loop(0, targets // CORES // CHIP_BLOCK, some_chips, 0)


def terms(level, core, cols, cols_other, panels, mine, other):
    targets = mine.shape[0]
    return pl.pallas_call(
        functools.partial(terms_kernel, level),
        out_shape=jax.ShapeDtypeStruct((targets // CORES, *panels.shape[1:]), jnp.bfloat16),
        in_specs=[SMEM, SMEM, SMEM, VMEM, VMEM, VMEM],
        out_specs=VMEM,
        compiler_params=PARAMS,
        name="level_terms",
    )(core, cols, cols_other, panels, mine, other)


def on_device(rhs, diag_inv, factor, columns):
    levels = rhs.shape[0]
    half = rhs.shape[-1] // CORES
    peers = lax.axis_size("row")
    here = lax.axis_index("core").astype(jnp.int32)
    core = here.reshape(1)
    swap = functools.partial(lax.ppermute, axis_name="core", perm=[(0, 1), (1, 0)])

    rhs_here = lax.dynamic_slice_in_dim(rhs[:, 0, 0], here * half, half, axis=2)
    rhs_other = swap(lax.dynamic_slice_in_dim(rhs[:, 0, 0], (1 - here) * half, half, axis=2))
    inv_other = swap(diag_inv)
    columns_other = swap(columns)
    large, rhs_other, inv_other, columns_other = lax.optimization_barrier(
        (factor, rhs_other, inv_other, columns_other)
    )
    factor_other = swap(large)
    ring = peers // RING_PARTS
    order = [part * ring + i for i in range(ring) for part in range(RING_PARTS)]
    cols, cols_other = (
        (x % ring * RING_PARTS + x // ring).reshape(-1) for x in (columns, columns_other)
    )
    rhs_all = (rhs_here, rhs_other)
    inv_all = (diag_inv[:, 0, 0], inv_other[:, 0, 0])

    first = [(x[0], y[0]) for x, y in zip(rhs_all, inv_all)]
    mine, other, copies = first_solve(
        core, jnp.stack([jnp.concatenate(x, axis=1) for x in first]), levels, peers
    )
    solved = (mine, other)
    first_factors = factor[0, 0, 0], factor_other[0, 0, 0]
    for level in range(levels - 1):
        panels = lax.all_to_all(
            copies, "row", 0, 0, axis_index_groups=[order], tiled=True
        )
        factors = (
            (factor[level, 0, 0], factor_other[level, 0, 0]) if level else first_factors
        )
        partial = terms(level, core, cols, cols_other, panels, *factors)
        received = lax.all_to_all(partial, "chip", 0, 0, tiled=True)
        last = level + 2 == levels
        solved, copies = solve(level + 1, received, rhs_all, inv_all, solved, 0 if last else peers)

    mine, other = solved[0], swap(solved[1])
    out = jnp.where(
        here == 0,
        jnp.concatenate([mine, other], axis=-1),
        jnp.concatenate([other, mine], axis=-1),
    )
    return out[:, None, None]


def solution(mesh):
    cols, rows = mesh.devices.shape
    fine = Mesh(mesh.devices.reshape(cols // CORES, CORES, rows), ("chip", "core", "row"))
    owner = ("chip", "core")
    return jax.shard_map(
        on_device,
        mesh=fine,
        in_specs=(
            P(None, owner, "row", None, None),
            P(None, owner, "row", None, None),
            P(None, owner, "row", None, None, None, None),
            P(None, owner, "row", None, None),
        ),
        out_specs=P(None, owner, "row", None, None),
        check_vma=False,
    )
```

```python
import functools

import jax
import jax.numpy as jnp
from jax import lax
from jax.experimental import pallas as pl
from jax.experimental.pallas import tpu as pltpu
from jax.sharding import Mesh
from jax.sharding import PartitionSpec as P

CORES = 2
RING_PARTS = 2
CHIP_BLOCK = 16
STAGGER = 30
VMEM_LIMIT = 16 * 1024 * 1024
VMEM = pl.BlockSpec(memory_space=pltpu.VMEM)
SMEM = pl.BlockSpec(memory_space=pltpu.SMEM)
PARAMS = pltpu.CompilerParams(vmem_limit_bytes=VMEM_LIMIT)


def times_inverse(inverse, remainder):
    high = remainder.astype(jnp.bfloat16)
    rest = remainder - high.astype(jnp.float32)
    middle = rest.astype(jnp.bfloat16)
    low = (rest - middle.astype(jnp.float32)).astype(jnp.bfloat16)
    dot = functools.partial(jnp.dot, inverse, preferred_element_type=jnp.float32)
    return (dot(low) + dot(middle) + dot(high)).astype(jnp.bfloat16)


def store_solved(level, slot, inverse, remainder, solved_ref, copies_ref):
    panel = times_inverse(inverse, remainder)
    solved_ref[level] = panel
    if copies_ref is not None:
        for peer in range(copies_ref.shape[0]):
            copies_ref[peer, slot] = panel


def first_kernel(core_ref, given_ref, mine_ref, other_ref, copies_ref):
    def once(_, carry):
        for slot, solved_ref in enumerate((mine_ref, other_ref)):
            half = solved_ref.shape[-1]
            remainder = given_ref[slot, :, :half].astype(jnp.float32)
            store_solved(0, slot, given_ref[slot, :, half:], remainder, solved_ref, copies_ref)
        return carry

    lax.fori_loop(0, 1 + (1 - core_ref[0]) * STAGGER, once, 0)


def next_kernel(level, terms_ref, *refs):
    rhs_refs, inv_refs, solved_refs = refs[:2], refs[2:4], refs[6:8]
    copies_ref = refs[8] if len(refs) > 8 else None
    for slot in range(CORES):
        total = terms_ref[0, slot].astype(jnp.float32)
        for chip in range(1, terms_ref.shape[0]):
            total += terms_ref[chip, slot].astype(jnp.float32)
        remainder = rhs_refs[slot][level].astype(jnp.float32) - total
        store_solved(level, slot, inv_refs[slot][level], remainder, solved_refs[slot], copies_ref)


def first_solve(core, given, levels, peers):
    _, blk, width = given.shape
    half = width - blk
    solved = jax.ShapeDtypeStruct((levels, blk, half), jnp.bfloat16)
    return pl.pallas_call(
        first_kernel,
        out_shape=(
            solved,
            solved,
            jax.ShapeDtypeStruct((peers, CORES, blk, half), jnp.bfloat16),
        ),
        in_specs=[SMEM, VMEM],
        out_specs=(VMEM, VMEM, VMEM),
        compiler_params=PARAMS,
        name="first_panels",
    )(core, given)


def solve(level, received, rhs, inv, solved, peers):
    outs = [jax.ShapeDtypeStruct(x.shape, x.dtype) for x in solved]
    if peers:
        outs.append(jax.ShapeDtypeStruct((peers, *received.shape[1:]), jnp.bfloat16))
    result = pl.pallas_call(
        functools.partial(next_kernel, level),
        out_shape=tuple(outs),
        in_specs=[VMEM] * 7,
        out_specs=(VMEM,) * len(outs),
        input_output_aliases={5: 0, 6: 1},
        compiler_params=PARAMS,
        name="solve_panels",
    )(received, *rhs, *inv, *solved)
    return result[:2], result[2] if peers else None


def terms_kernel(level, core_ref, cols_ref, cols_other_ref, panels_ref, mine_ref, other_ref, out_ref):
    core = core_ref[0]
    targets, slots = mine_ref.shape[:2]

    def some_chips(block, carry):
        for chip in range(CHIP_BLOCK):
            for slot in range(CORES):
                target = CORES * (block * CHIP_BLOCK + chip) + (core if slot == 0 else 1 - core)
                place = (level * targets + target) * slots
                left, right = [], []
                for which, (blocks, cols) in enumerate(
                    ((mine_ref, cols_ref), (other_ref, cols_other_ref))
                ):
                    for m in range(slots):
                        left.append(blocks[target, m])
                        right.append(panels_ref[cols[place + m], which])
                product = jnp.dot(
                    jnp.concatenate(left, axis=1),
                    jnp.concatenate(right, axis=0),
                    preferred_element_type=jnp.float32,
                )
                out_ref[block * CHIP_BLOCK + chip, slot] = product.astype(jnp.bfloat16)
        return carry

    lax.fori_loop(0, targets // CORES // CHIP_BLOCK, some_chips, 0)


def terms(level, core, cols, cols_other, panels, mine, other):
    targets = mine.shape[0]
    return pl.pallas_call(
        functools.partial(terms_kernel, level),
        out_shape=jax.ShapeDtypeStruct((targets // CORES, *panels.shape[1:]), jnp.bfloat16),
        in_specs=[SMEM, SMEM, SMEM, VMEM, VMEM, VMEM],
        out_specs=VMEM,
        compiler_params=PARAMS,
        name="level_terms",
    )(core, cols, cols_other, panels, mine, other)


def on_device(rhs, diag_inv, factor, columns):
    levels = rhs.shape[0]
    half = rhs.shape[-1] // CORES
    peers = lax.axis_size("row")
    here = lax.axis_index("core").astype(jnp.int32)
    core = here.reshape(1)
    swap = functools.partial(lax.ppermute, axis_name="core", perm=[(0, 1), (1, 0)])

    rhs_here = lax.dynamic_slice_in_dim(rhs[:, 0, 0], here * half, half, axis=2)
    rhs_other = swap(lax.dynamic_slice_in_dim(rhs[:, 0, 0], (1 - here) * half, half, axis=2))
    inv_other = swap(diag_inv)
    columns_other = swap(columns)
    large, rhs_other, inv_other, columns_other = lax.optimization_barrier(
        (factor, rhs_other, inv_other, columns_other)
    )
    factor_other = swap(large)
    ring = peers // RING_PARTS
    order = [part * ring + i for i in range(ring) for part in range(RING_PARTS)]
    cols, cols_other = (
        (x % ring * RING_PARTS + x // ring).reshape(-1) for x in (columns, columns_other)
    )
    rhs_all = (rhs_here, rhs_other)
    inv_all = (diag_inv[:, 0, 0], inv_other[:, 0, 0])

    first = [(x[0], y[0]) for x, y in zip(rhs_all, inv_all)]
    mine, other, copies = first_solve(
        core, jnp.stack([jnp.concatenate(x, axis=1) for x in first]), levels, peers
    )
    solved = (mine, other)
    first_factors = factor[0, 0, 0], factor_other[0, 0, 0]
    for level in range(levels - 1):
        panels = lax.all_to_all(
            copies, "row", 0, 0, axis_index_groups=[order], tiled=True
        )
        factors = (
            (factor[level, 0, 0], factor_other[level, 0, 0]) if level else first_factors
        )
        partial = terms(level, core, cols, cols_other, panels, *factors)
        received = lax.all_to_all(partial, "chip", 0, 0, tiled=True)
        last = level + 2 == levels
        solved, copies = solve(level + 1, received, rhs_all, inv_all, solved, 0 if last else peers)

    mine, other = solved[0], swap(solved[1])
    out = jnp.where(
        here == 0,
        jnp.concatenate([mine, other], axis=-1),
        jnp.concatenate([other, mine], axis=-1),
    )
    return out[:, None, None]


def solution(mesh):
    cols, rows = mesh.devices.shape
    fine = Mesh(mesh.devices.reshape(cols // CORES, CORES, rows), ("chip", "core", "row"))
    owner = ("chip", "core")
    return jax.shard_map(
        on_device,
        mesh=fine,
        in_specs=(
            P(None, owner, "row", None, None),
            P(None, owner, "row", None, None),
            P(None, owner, "row", None, None, None, None),
            P(None, owner, "row", None, None),
        ),
        out_specs=P(None, owner, "row", None, None),
        check_vma=False,
    )
```
